32 devices in a mesh: gx: 8 (over y, x, core), gy: 4 (over z).
Axes of the slice: x: 2, y: 2, z: 4, core: 2. Of those that a mesh axis runs over, the one named last changes fastest.
Arguments:
- concentration: bfloat16 [128, 128, 512], P(None, 'gx', 'gy'), may hold values from 0.099609375 to 1
- adjoint_next: bfloat16 [128, 128, 512], P(None, 'gx', 'gy'), may hold values from 0 to 2
- sign_x: int32 [128, 512], P('gx', 'gy'), may hold values from 0 to 1
- sign_y: int32 [128, 512], P('gx', 'gy'), may hold values from 0 to 1
- courant_x: float32 [128, 512], P('gx', 'gy'), may hold values from 0.05 to 0.24
- courant_y: float32 [128, 512], P('gx', 'gy'), may hold values from 0.05 to 0.24
- active: int32 [128, 512], P('gx', 'gy'), may hold values from 0 to 1, as said below
- kernel_a: float32 [128], replicated, may hold values from 0.01 to 0.1
- kernel_b: float32 [128], replicated, may hold values from 0.01 to 0.1
Outputs:
- gradient: float32 [128, 128, 512], P(None, 'gx', 'gy')
The draws below stay inside these ranges and needn't reach their ends.
Inputs may be any that keep to these rules, and one draw needn't show every extreme that they name: Among the devices that share one gy index, 2 hold exactly 2048 active cells (all of their cells) and the others exactly 256; which devices hold more is drawn anew.
All inputs are finite; a program needn't handle non-finite values.
Results may differ from the reference program's by a relative error of at most 0.0003.
Values sent between devices are 32-bit elements; how exact they have to be, the bound alone decides.
A program may use at most 64 MiB of HBM per device.

```python
import math
import jax
import jax.numpy as jnp
from jax import lax

NB = 128
SUBSTEPS = 4
CX = 16
CY = 128
NX = 128
NY = 512
N_GX = 8
N_GY = 4


def draw_active(key, part):
    first_key, second_key = jax.random.split(key)
    busy_rank = jax.vmap(lambda subkey: jax.random.permutation(subkey, N_GX))(jax.random.split(first_key, N_GY))
    cell_total = CX * CY
    quota_cells = jnp.where(busy_rank < N_GX // 4, cell_total, cell_total // 8)
    shuffled = jax.vmap(lambda subkey: jax.random.permutation(subkey, cell_total))(jax.random.split(second_key, N_GY * N_GX))
    shuffled = shuffled.reshape(N_GY, N_GX, cell_total)
    chosen = (shuffled < quota_cells[:, :, None]).astype(jnp.int32)
    chosen = chosen.reshape(N_GY, N_GX, CX, CY).transpose(1, 2, 0, 3).reshape(N_GX * CX, N_GY * CY)
    return chosen


def touch_ends(drawn, stream_key, low, top_value):
    shape = drawn.shape
    place = [jax.random.randint(jax.random.fold_in(stream_key, axis), (), 0, shape[axis]) for axis in range(len(shape))]
    drawn = drawn.at[tuple(place)].set(low)
    longest = shape.index(max(shape))
    place[longest] = (place[longest] + 1) % shape[longest]
    return drawn.at[tuple(place)].set(top_value)


def level_of(own_key, shape, shards, smallest, high):
    def one(axis_at, parts):
        draws = jax.random.uniform(jax.random.fold_in(jax.random.fold_in(own_key, 6), axis_at), (parts,), jnp.float32, smallest / len(shards), high / len(shards))
        return jnp.repeat(jnp.exp(draws), shape[axis_at] // parts).reshape((-1,) + (1,) * (len(shape) - axis_at - 1))

    level = one(*shards[0])
    for cut in shards[1:]:
        level = level * one(*cut)
    return level


def setup_inputs(seed: int = 0) -> dict:
    key_of = jax.random.split(jax.random.key(seed), 10)
    return {
        "concentration": jnp.clip(jnp.exp(math.log(1.0) - 2.306499 * jax.random.uniform(key_of[0], (NB, NX, NY), jnp.float32) ** level_of(key_of[0], (NB, NX, NY), ((1, 8), (2, 4)), -0.2, 0.2)), 0.099609375, 1.0).astype(jnp.bfloat16),
        "adjoint_next": jnp.clip(2.0 * jax.random.uniform(key_of[1], (NB, NX, NY), jnp.float32) ** level_of(key_of[1], (NB, NX, NY), ((1, 8), (2, 4)), -0.2, 0.2), 0.0, 2.0).astype(jnp.bfloat16),
        "sign_x": touch_ends(jax.random.randint(key_of[2], (NX, NY), 0, 2), jax.random.fold_in(key_of[2], 1), 0, 1).astype(jnp.int32),
        "sign_y": touch_ends(jax.random.randint(key_of[3], (NX, NY), 0, 2), jax.random.fold_in(key_of[3], 1), 0, 1).astype(jnp.int32),
        "courant_x": jnp.clip(0.05 + 0.19 * jax.random.uniform(key_of[4], (NX, NY), jnp.float32) ** level_of(key_of[4], (NX, NY), ((0, 8), (1, 4)), -0.2, 0.2), 0.05, 0.24),
        "courant_y": jnp.clip(0.05 + 0.19 * jax.random.uniform(key_of[5], (NX, NY), jnp.float32) ** level_of(key_of[5], (NX, NY), ((0, 8), (1, 4)), -0.2, 0.2), 0.05, 0.24),
        "active": draw_active(jax.random.fold_in(key_of[9], 71), 0),
        "kernel_a": jnp.clip(jnp.exp(jax.random.uniform(key_of[7], (NB,), jnp.float32, math.log(0.01), math.log(0.1))), 0.01, 0.1),
        "kernel_b": jnp.clip(jnp.exp(jax.random.uniform(key_of[8], (NB,), jnp.float32, math.log(0.01), math.log(0.1))), 0.01, 0.1),
    }


def face_weights(sign_x, sign_y, courant_x, courant_y):
    plus_x = sign_x.astype(jnp.float32)
    plus_y = sign_y.astype(jnp.float32)
    column = jnp.arange(NY, dtype=jnp.int32)[None, :]
    inside = (column > 0).astype(jnp.float32)
    return (courant_x * plus_x, courant_x * (1.0 - plus_x), courant_y * plus_y * inside, courant_y * (1.0 - plus_y) * inside)


def after_x(field):
    return jnp.roll(field, -1, axis=-2)


def before_x(field):
    return jnp.roll(field, 1, axis=-2)


def after_y(field):
    return jnp.concatenate([field[..., 1:], jnp.zeros_like(field[..., :1])], axis=-1)


def before_y(field):
    return jnp.concatenate([jnp.zeros_like(field[..., :1]), field[..., :-1]], axis=-1)


def transport_forward(field, weights):
    upward_x, backward_x, upward_y, backward_y = weights
    return (field + upward_x * before_x(field) - (backward_x + after_x(upward_x)) * field + after_x(backward_x) * after_x(field)
            + upward_y * before_y(field) - (backward_y + after_y(upward_y)) * field + after_y(backward_y) * after_y(field))


def transport_adjoint(field, weights):
    upward_x, backward_x, upward_y, backward_y = weights
    return (field * (1.0 - backward_x - after_x(upward_x) - backward_y - after_y(upward_y))
            + after_x(upward_x) * after_x(field) + backward_x * before_x(field)
            + after_y(upward_y) * after_y(field) + backward_y * before_y(field))


def spectrum(values):
    return jnp.fft.rfft(values, n=2 * NB, axis=0)


def gain_terms(spectra_a, spectra_b):
    full = jnp.fft.irfft(spectra_a * spectra_b, n=2 * NB, axis=0)
    return jnp.concatenate([jnp.zeros_like(full[:1]), full[:NB - 1]], axis=0)


def lag_terms(spectra_l, spectra_v):
    full = jnp.fft.irfft(spectra_l * jnp.conj(spectra_v), n=2 * NB, axis=0)
    return full[1:NB + 1]


def coagulation(column_state, column_adjoint, mask_row, kernel_a, kernel_b):
    weight_a = kernel_a[:, None]
    weight_b = kernel_b[:, None]
    current = column_state
    saved = []
    for substep in range(SUBSTEPS):
        scaled_a = weight_a * current
        scaled_b = weight_b * current
        spectra_a = spectrum(scaled_a)
        spectra_b = spectrum(scaled_b)
        total_a = jnp.sum(scaled_a, axis=0, keepdims=True)
        total_b = jnp.sum(scaled_b, axis=0, keepdims=True)
        saved.append((current, spectra_a, spectra_b, total_a, total_b))
        if substep < SUBSTEPS - 1:
            gained = gain_terms(spectra_a, spectra_b)
            current = current + mask_row * (gained - current * (weight_a * total_b + weight_b * total_a))
    adjoint = column_adjoint
    for substep in reversed(range(SUBSTEPS)):
        current, spectra_a, spectra_b, total_a, total_b = saved[substep]
        spectra_l = spectrum(adjoint)
        grad_a = lag_terms(spectra_l, spectra_b)
        grad_b = lag_terms(spectra_l, spectra_a)
        moment_a = jnp.sum(adjoint * current * weight_a, axis=0, keepdims=True)
        moment_b = jnp.sum(adjoint * current * weight_b, axis=0, keepdims=True)
        change = (weight_a * grad_a + weight_b * grad_b - adjoint * (weight_a * total_b + weight_b * total_a)
                  - weight_b * moment_a - weight_a * moment_b)
        adjoint = adjoint + mask_row * change
    return adjoint


def reference(concentration, adjoint_next, sign_x, sign_y, courant_x, courant_y, active, kernel_a, kernel_b):
    weights = face_weights(sign_x, sign_y, courant_x, courant_y)
    moved = transport_forward(concentration.astype(jnp.float32), weights)
    adjoint_end = adjoint_next.astype(jnp.float32)
    mask_all = active.astype(jnp.float32)

    def one_row(packed):
        row_state, row_adjoint, row_mask = packed
        return coagulation(row_state, row_adjoint, row_mask[None, :], kernel_a, kernel_b)

    rows_out = lax.map(one_row, (jnp.moveaxis(moved, 1, 0), jnp.moveaxis(adjoint_end, 1, 0), mask_all))
    adjoint_mid = jnp.moveaxis(rows_out, 0, 1)
    return transport_adjoint(adjoint_mid, weights)
```

```python
import functools

import jax
import jax.numpy as jnp
import numpy as np
from jax import lax
from jax.experimental import pallas as pl
from jax.experimental.pallas import tpu as pltpu
from jax.sharding import PartitionSpec as P

SUBSTEPS = 4
F32 = jnp.float32
BF16 = jnp.bfloat16


def dft_tables(bins):
    freq = 2 * np.arange(bins) + 1
    index = np.arange(bins)
    angle = np.pi * (freq[:, None] * index[None, :] % (4 * bins)) / (2 * bins)
    forward = np.concatenate([np.cos(angle), -np.sin(angle)], axis=0)

    def inverse(outputs):
        phase = np.pi * (outputs[:, None] * freq[None, :] % (4 * bins)) / (2 * bins)
        return np.concatenate([np.cos(phase), -np.sin(phase)], axis=1) / bins

    gain = inverse(index - 1) * (index > 0)[:, None]
    lag = inverse(index + 1)
    return tuple(np.asarray(t, np.float32) for t in (forward, gain, lag))


def split(values):
    high = values.astype(BF16)
    low = (values - high.astype(F32)).astype(BF16)
    return high, low


def stacked(values):
    high, low = split(values)
    return jnp.concatenate([high, low, high], axis=0)


def table3(values):
    high, low = split(values)
    return jnp.concatenate([high, high, low], axis=1)


def dot(table, values):
    return jnp.dot(table, values, preferred_element_type=F32)


def product(left, right):
    half = left.shape[0] // 2
    lr, li, rr, ri = left[:half], left[half:], right[:half], right[half:]
    return jnp.concatenate([lr * rr - li * ri, lr * ri + li * rr], axis=0)


def product_conj(left, right):
    half = left.shape[0] // 2
    lr, li, rr, ri = left[:half], left[half:], right[:half], right[half:]
    return jnp.concatenate([lr * rr + li * ri, li * rr - lr * ri], axis=0)


def kernel(
    n_gx, n_gy, width_x,
    conc, adj, sx, sy, cx, cy, active, ka_ref, kb_ref, fwd_ref, gain_ref, lag_ref,
    out,
    wide, wide_adj, state, lam, y_send, y_recv, z_send, z_recv, moved, faces, t_fwd, t_gain, t_lam, t_lag,
    send_sem, recv_sem,
):
    bins = ka_ref.shape[1]
    width_y = sx.shape[1]
    gx = lax.axis_index("gx")
    gy = lax.axis_index("gy")
    nxt_x, prv_x = lax.rem(gx + 1, n_gx), lax.rem(gx + n_gx - 1, n_gx)
    nxt_y, prv_y = jnp.minimum(gy + 1, n_gy - 1), jnp.maximum(gy - 1, 0)
    has_prv, has_nxt = gy > 0, gy < n_gy - 1
    mesh_id = pl.DeviceIdType.MESH

    barrier = pltpu.get_barrier_semaphore()
    pl.semaphore_signal(barrier, inc=1, device_id=(prv_x, gy), device_id_type=mesh_id)
    pl.semaphore_signal(barrier, inc=1, device_id=(nxt_x, gy), device_id_type=mesh_id)

    @pl.when(has_prv)
    def _():
        pl.semaphore_signal(barrier, inc=1, device_id=(gx, prv_y), device_id_type=mesh_id)

    @pl.when(has_nxt)
    def _():
        pl.semaphore_signal(barrier, inc=1, device_id=(gx, nxt_y), device_id_type=mesh_id)

    lane = lax.broadcasted_iota(jnp.int32, (bins, width_y), 1)
    lane_x = lax.broadcasted_iota(jnp.int32, (width_x, width_y), 1)

    plus_x = sx[...].astype(F32)
    plus_y = sy[...].astype(F32)
    inside = (lane_x + gy * width_y > 0).astype(F32)
    ux = cx[...] * plus_x
    bx = cx[...] * (1.0 - plus_x)
    uy = cy[...] * plus_y * inside
    by = cy[...] * (1.0 - plus_y) * inside

    wide[...] = conc[...].astype(F32)
    for x in range(width_x):
        state[x + 1, :bins, :] = wide[pl.ds(x, bins, stride=width_x), :]
    state[1, bins:bins + 1, :] = ux[0:1]
    state[1, bins + 1:bins + 2, :] = bx[0:1]
    state[1, bins + 2:, :] = jnp.zeros((6, width_y), F32)
    state[width_x, bins:, :] = jnp.zeros((8, width_y), F32)

    def edges(field, buffer):
        to_prv = jnp.zeros((bins, width_y), F32)
        to_nxt = jnp.zeros((bins, width_y), F32)
        for x in range(width_x):
            slab = field[x + 1, :bins, :]
            at_low = pltpu.roll(slab, x, 1) if x else slab
            to_prv = jnp.where(lane == x, at_low, to_prv)
            to_nxt = jnp.where(lane == x, pltpu.roll(slab, x + 1, 1), to_nxt)
        buffer[0, :bins, :] = to_prv
        buffer[1, :bins, :] = to_nxt

    edges(state, y_send)
    y_send[0, bins:bins + width_x, :] = uy
    y_send[0, bins + width_x:, :] = by
    y_send[1, bins:, :] = jnp.zeros((2 * width_x, width_y), F32)

    def x_copies(field, base):
        return (
            pltpu.make_async_remote_copy(
                src_ref=field.at[1], dst_ref=field.at[width_x + 1],
                send_sem=send_sem.at[base], recv_sem=recv_sem.at[base],
                device_id=(prv_x, gy), device_id_type=mesh_id),
            pltpu.make_async_remote_copy(
                src_ref=field.at[width_x], dst_ref=field.at[0],
                send_sem=send_sem.at[base + 1], recv_sem=recv_sem.at[base + 1],
                device_id=(nxt_x, gy), device_id_type=mesh_id),
        )

    def y_copies(source, target, base):
        return (
            pltpu.make_async_remote_copy(
                src_ref=source.at[0], dst_ref=target.at[1],
                send_sem=send_sem.at[base], recv_sem=recv_sem.at[base],
                device_id=(gx, prv_y), device_id_type=mesh_id),
            pltpu.make_async_remote_copy(
                src_ref=source.at[1], dst_ref=target.at[0],
                send_sem=send_sem.at[base + 1], recv_sem=recv_sem.at[base + 1],
                device_id=(gx, nxt_y), device_id_type=mesh_id),
        )

    def start_y(copies, target):
        to_prv, to_nxt = copies

        @pl.when(has_prv)
        def _():
            to_prv.start()

        @pl.when(has_nxt)
        def _():
            to_nxt.start()

        @pl.when(jnp.logical_not(has_prv))
        def _():
            target[0] = jnp.zeros(target.shape[1:], F32)

        @pl.when(jnp.logical_not(has_nxt))
        def _():
            target[1] = jnp.zeros(target.shape[1:], F32)

    def wait_y(copies):
        to_prv, to_nxt = copies

        @pl.when(has_prv)
        def _():
            to_prv.wait_send()
            to_nxt.wait_recv()

        @pl.when(has_nxt)
        def _():
            to_nxt.wait_send()
            to_prv.wait_recv()

    pl.semaphore_wait(barrier, 2 + has_prv.astype(jnp.int32) + has_nxt.astype(jnp.int32))
    first_x = x_copies(state, 0)
    first_y = y_copies(y_send, y_recv, 2)
    start_y(first_y, y_recv)
    for copy in first_x:
        copy.start()

    ka_row, kb_row = ka_ref[...], kb_ref[...]
    ka_full = jnp.broadcast_to(ka_row, (bins, bins))
    kb_full = jnp.broadcast_to(kb_row, (bins, bins))
    ka_col, kb_col = ka_full.T, kb_full.T
    pair = ka_col * kb_full + kb_col * ka_full
    forward = fwd_ref[...]
    t_fwd[0:2 * bins, :] = table3(forward * ka_row)
    t_fwd[2 * bins:4 * bins, :] = table3(forward * kb_row)
    t_fwd[4 * bins:, :] = table3(pair)
    t_gain[...] = table3(gain_ref[...])
    t_lam[...] = table3(forward)
    lag = lag_ref[...]
    ka_col2 = jnp.concatenate([ka_col, ka_col], axis=1)
    kb_col2 = jnp.concatenate([kb_col, kb_col], axis=1)
    t_lag[:, :6 * bins] = table3(ka_col2 * lag)
    t_lag[:, 6 * bins:12 * bins] = table3(kb_col2 * lag)
    t_lag[:, 12 * bins:] = table3(-pair)

    wide_adj[...] = adj[...].astype(F32)

    wait_y(first_y)
    for copy in first_x:
        copy.wait()

    ux_next = jnp.concatenate([ux[1:], state[width_x + 1, bins:bins + 1, :]], axis=0)
    bx_next = jnp.concatenate([bx[1:], state[width_x + 1, bins + 1:bins + 2, :]], axis=0)
    last_lane = lane_x == width_y - 1
    uy_next = jnp.where(
        last_lane, pltpu.roll(y_recv[1, bins:bins + width_x, :], width_y - 1, 1), pltpu.roll(uy, width_y - 1, 1))
    by_next = jnp.where(
        last_lane, pltpu.roll(y_recv[1, bins + width_x:, :], width_y - 1, 1), pltpu.roll(by, width_y - 1, 1))
    centre = 1.0 - bx - ux_next - by - uy_next
    for index, values in enumerate((centre, ux, bx, ux_next, bx_next, uy, by, uy_next, by_next)):
        faces[index] = values

    def stencil(field, halo, x, low_x, high_x, low_y, high_y):
        slab = field[x + 1, :bins, :]
        before = jnp.where(lane == 0, pltpu.roll(halo[0, :bins, :], (width_y - x) % width_y, 1), pltpu.roll(slab, 1, 1))
        after = jnp.where(
            lane == width_y - 1, pltpu.roll(halo[1, :bins, :], width_y - 1 - x, 1), pltpu.roll(slab, width_y - 1, 1))
        row = lambda k: faces[k, x:x + 1, :]
        return (
            slab * row(0)
            + row(low_x) * field[x, :bins, :]
            + row(high_x) * field[x + 2, :bins, :]
            + row(low_y) * before
            + row(high_y) * after
        )

    for x in range(width_x):
        moved[x] = stencil(state, y_recv, x, 1, 4, 5, 8)
        lam[x + 1, :bins, :] = wide_adj[pl.ds(x, bins, stride=width_x), :]

    def coagulate(first, second):
        current = jnp.concatenate([moved[first], moved[second]], axis=1)
        start = jnp.concatenate([lam[first + 1, :bins, :], lam[second + 1, :bins, :]], axis=1)
        saved = []
        for step in range(SUBSTEPS):
            spectra = dot(t_fwd[...], stacked(current))
            loss = spectra[4 * bins:]
            saved.append((current, spectra, loss))
            if step < SUBSTEPS - 1:
                both = product(spectra[:2 * bins], spectra[2 * bins:4 * bins])
                current = current + dot(t_gain[...], stacked(both)) - current * loss
        adjoint = start
        for step in reversed(range(SUBSTEPS)):
            current, spectra, loss = saved[step]
            spectra_l = dot(t_lam[...], stacked(adjoint))
            with_b = product_conj(spectra_l, spectra[2 * bins:4 * bins])
            with_a = product_conj(spectra_l, spectra[:2 * bins])
            terms = jnp.concatenate([stacked(with_b), stacked(with_a), stacked(adjoint * current)], axis=0)
            adjoint = adjoint + dot(t_lag[...], terms) - adjoint * loss
        on = jnp.concatenate([active[pl.ds(first, 1), :], active[pl.ds(second, 1), :]], axis=1) == 1
        result = jnp.where(on, adjoint, start)
        lam[first + 1, :bins, :] = result[:, :width_y]
        lam[second + 1, :bins, :] = result[:, width_y:]

    coagulate(0, width_x - 1)
    lam[1, bins:, :] = jnp.zeros((8, width_y), F32)
    lam[width_x, bins:, :] = jnp.zeros((8, width_y), F32)
    second_x = x_copies(lam, 4)
    for copy in second_x:
        copy.start()

    @pl.loop(0, width_x // 2 - 1)
    def _(block):
        coagulate(2 * block + 1, 2 * block + 2)

    edges(lam, z_send)
    second_y = y_copies(z_send, z_recv, 6)
    start_y(second_y, z_recv)
    for copy in second_x:
        copy.wait()
    wait_y(second_y)
    for x in range(width_x):
        out[pl.ds(x, bins, stride=width_x), :] = stencil(lam, z_recv, x, 2, 3, 6, 7)


def body(n_gx, n_gy, concentration, adjoint_next, sign_x, sign_y, courant_x, courant_y, active, kernel_a, kernel_b):
    bins, width_x, width_y = concentration.shape
    rows = bins * width_x
    tables = dft_tables(bins)
    vmem = pl.BlockSpec(memory_space=pltpu.VMEM)
    result = pl.pallas_call(
        functools.partial(kernel, n_gx, n_gy, width_x),
        out_shape=jax.ShapeDtypeStruct((rows, width_y), F32),
        in_specs=[vmem] * 12,
        out_specs=vmem,
        scratch_shapes=[
            pltpu.VMEM((rows, width_y), F32),
            pltpu.VMEM((rows, width_y), F32),
            pltpu.VMEM((width_x + 2, bins + 8, width_y), F32),
            pltpu.VMEM((width_x + 2, bins + 8, width_y), F32),
            pltpu.VMEM((2, bins + 2 * width_x, width_y), F32),
            pltpu.VMEM((2, bins + 2 * width_x, width_y), F32),
            pltpu.VMEM((2, bins, width_y), F32),
            pltpu.VMEM((2, bins, width_y), F32),
            pltpu.VMEM((width_x, bins, width_y), F32),
            pltpu.VMEM((9, width_x, width_y), F32),
            pltpu.VMEM((5 * bins, 3 * bins), BF16),
            pltpu.VMEM((bins, 6 * bins), BF16),
            pltpu.VMEM((2 * bins, 3 * bins), BF16),
            pltpu.VMEM((bins, 15 * bins), BF16),
            pltpu.SemaphoreType.DMA((8,)),
            pltpu.SemaphoreType.DMA((8,)),
        ],
        compiler_params=pltpu.CompilerParams(
            collective_id=0, has_side_effects=True, vmem_limit_bytes=48 * 1024 * 1024
        ),
    )(
        concentration.reshape(rows, width_y),
        adjoint_next.reshape(rows, width_y),
        sign_x, sign_y, courant_x, courant_y, active,
        kernel_a.reshape(1, bins), kernel_b.reshape(1, bins),
        *(jnp.asarray(t) for t in tables),
    )
    return result.reshape(bins, width_x, width_y)


def solution(mesh):
    return jax.shard_map(
        functools.partial(body, mesh.shape["gx"], mesh.shape["gy"]),
        mesh=mesh,
        in_specs=(
            P(None, "gx", "gy"),
            P(None, "gx", "gy"),
            P("gx", "gy"),
            P("gx", "gy"),
            P("gx", "gy"),
            P("gx", "gy"),
            P("gx", "gy"),
            P(),
            P(),
        ),
        out_specs=P(None, "gx", "gy"),
        check_vma=False,
    )
```

```python
import functools

import jax
import jax.numpy as jnp
import numpy as np
from jax import lax
from jax.experimental import pallas as pl
from jax.experimental.pallas import tpu as pltpu
from jax.sharding import PartitionSpec as P

SUBSTEPS = 4
F32 = jnp.float32
BF16 = jnp.bfloat16


def dft_tables(bins):
    freq = 2 * np.arange(bins) + 1
    index = np.arange(bins)
    angle = np.pi * (freq[:, None] * index[None, :] % (4 * bins)) / (2 * bins)
    forward = np.concatenate([np.cos(angle), -np.sin(angle)], axis=0)

    def inverse(outputs):
        phase = np.pi * (outputs[:, None] * freq[None, :] % (4 * bins)) / (2 * bins)
        return np.concatenate([np.cos(phase), -np.sin(phase)], axis=1) / bins

    gain = inverse(index - 1) * (index > 0)[:, None]
    lag = inverse(index + 1)
    return tuple(np.asarray(t, np.float32) for t in (forward, gain, lag))


def split(values):
    high = values.astype(BF16)
    low = (values - high.astype(F32)).astype(BF16)
    return high, low


def stacked(values):
    high, low = split(values)
    return jnp.concatenate([high, low, high], axis=0)


def table3(values):
    high, low = split(values)
    return jnp.concatenate([high, high, low], axis=1)


def dot(table, values):
    return jnp.dot(table, values, preferred_element_type=F32)


def product(left, right):
    half = left.shape[0] // 2
    lr, li, rr, ri = left[:half], left[half:], right[:half], right[half:]
    return jnp.concatenate([lr * rr - li * ri, lr * ri + li * rr], axis=0)


def product_conj(left, right):
    half = left.shape[0] // 2
    lr, li, rr, ri = left[:half], left[half:], right[:half], right[half:]
    return jnp.concatenate([lr * rr + li * ri, li * rr - lr * ri], axis=0)


def kernel(
    n_gx, n_gy, width_x,
    *refs,
):
    inputs, refs = refs[:12], refs[12:]
    out, refs = refs[0], refs[1:]
    fetched, refs = refs[:12], refs[12:]
    conc, adj, sx, sy, cx, cy, active, ka_ref, kb_ref, fwd_ref, gain_ref, lag_ref = fetched
    (wide, wide_adj, state, lam, y_send, y_recv, z_send, z_recv, moved, faces, t_fwd, t_gain, t_lam, t_lag,
     send_sem, recv_sem, in_sem, out_sem) = refs
    fetches = [pltpu.make_async_copy(i, f, in_sem.at[k]) for k, (i, f) in enumerate(zip(inputs, fetched))]
    for k in (0, 2, 3, 4, 5, 1, 7, 8, 9, 10, 11, 6):
        fetches[k].start()
    bins = ka_ref.shape[1]
    width_y = sx.shape[1]
    gx = lax.axis_index("gx")
    gy = lax.axis_index("gy")
    nxt_x, prv_x = lax.rem(gx + 1, n_gx), lax.rem(gx + n_gx - 1, n_gx)
    nxt_y, prv_y = jnp.minimum(gy + 1, n_gy - 1), jnp.maximum(gy - 1, 0)
    has_prv, has_nxt = gy > 0, gy < n_gy - 1
    mesh_id = pl.DeviceIdType.MESH

    barrier = pltpu.get_barrier_semaphore()
    pl.semaphore_signal(barrier, inc=1, device_id=(prv_x, gy), device_id_type=mesh_id)
    pl.semaphore_signal(barrier, inc=1, device_id=(nxt_x, gy), device_id_type=mesh_id)

    @pl.when(has_prv)
    def _():
        pl.semaphore_signal(barrier, inc=1, device_id=(gx, prv_y), device_id_type=mesh_id)

    @pl.when(has_nxt)
    def _():
        pl.semaphore_signal(barrier, inc=1, device_id=(gx, nxt_y), device_id_type=mesh_id)

    lane = lax.broadcasted_iota(jnp.int32, (bins, width_y), 1)
    lane_x = lax.broadcasted_iota(jnp.int32, (width_x, width_y), 1)

    for k in (2, 3, 4, 5):
        fetches[k].wait()
    plus_x = sx[...].astype(F32)
    plus_y = sy[...].astype(F32)
    inside = (lane_x + gy * width_y > 0).astype(F32)
    ux = cx[...] * plus_x
    bx = cx[...] * (1.0 - plus_x)
    uy = cy[...] * plus_y * inside
    by = cy[...] * (1.0 - plus_y) * inside

    fetches[0].wait()
    wide[...] = conc[...].astype(F32)
    for x in range(width_x):
        state[x + 1, :bins, :] = wide[pl.ds(x, bins, stride=width_x), :]
    state[1, bins:bins + 1, :] = ux[0:1]
    state[1, bins + 1:bins + 2, :] = bx[0:1]
    state[1, bins + 2:, :] = jnp.zeros((6, width_y), F32)
    state[width_x, bins:, :] = jnp.zeros((8, width_y), F32)

    def edges(field, places):
        to_prv = jnp.zeros((bins, width_y), F32)
        to_nxt = jnp.zeros((bins, width_y), F32)
        for x in places:
            slab = field[x + 1, :bins, :]
            to_prv = jnp.where(lane == x, pltpu.roll(slab, x, 1), to_prv)
            to_nxt = jnp.where(lane == x, pltpu.roll(slab, x + 1, 1), to_nxt)
        return to_prv, to_nxt

    y_send[0, :bins, :], y_send[1, :bins, :] = edges(state, range(width_x))
    y_send[0, bins:bins + width_x, :] = uy
    y_send[0, bins + width_x:, :] = by
    y_send[1, bins:, :] = jnp.zeros((2 * width_x, width_y), F32)

    def x_copies(field, base):
        return (
            pltpu.make_async_remote_copy(
                src_ref=field.at[1], dst_ref=field.at[width_x + 1],
                send_sem=send_sem.at[base], recv_sem=recv_sem.at[base],
                device_id=(prv_x, gy), device_id_type=mesh_id),
            pltpu.make_async_remote_copy(
                src_ref=field.at[width_x], dst_ref=field.at[0],
                send_sem=send_sem.at[base + 1], recv_sem=recv_sem.at[base + 1],
                device_id=(nxt_x, gy), device_id_type=mesh_id),
        )

    def y_copies(source, target, base):
        return (
            pltpu.make_async_remote_copy(
                src_ref=source.at[0], dst_ref=target.at[1],
                send_sem=send_sem.at[base], recv_sem=recv_sem.at[base],
                device_id=(gx, prv_y), device_id_type=mesh_id),
            pltpu.make_async_remote_copy(
                src_ref=source.at[1], dst_ref=target.at[0],
                send_sem=send_sem.at[base + 1], recv_sem=recv_sem.at[base + 1],
                device_id=(gx, nxt_y), device_id_type=mesh_id),
        )

    def start_y(copies, target):
        to_prv, to_nxt = copies

        @pl.when(has_prv)
        def _():
            to_prv.start()

        @pl.when(has_nxt)
        def _():
            to_nxt.start()

        @pl.when(jnp.logical_not(has_prv))
        def _():
            target[0] = jnp.zeros(target.shape[1:], F32)

        @pl.when(jnp.logical_not(has_nxt))
        def _():
            target[1] = jnp.zeros(target.shape[1:], F32)

    def wait_y(copies):
        to_prv, to_nxt = copies

        @pl.when(has_prv)
        def _():
            to_prv.wait_send()
            to_nxt.wait_recv()

        @pl.when(has_nxt)
        def _():
            to_nxt.wait_send()
            to_prv.wait_recv()

    pl.semaphore_wait(barrier, 2 + has_prv.astype(jnp.int32) + has_nxt.astype(jnp.int32))
    first_x = x_copies(state, 0)
    first_y = y_copies(y_send, y_recv, 2)
    start_y(first_y, y_recv)
    for copy in first_x:
        copy.start()

    for k in (7, 8, 9, 10, 11):
        fetches[k].wait()
    ka_row, kb_row = ka_ref[...], kb_ref[...]
    ka_full = jnp.broadcast_to(ka_row, (bins, bins))
    kb_full = jnp.broadcast_to(kb_row, (bins, bins))
    ka_col, kb_col = ka_full.T, kb_full.T
    pair = ka_col * kb_full + kb_col * ka_full
    forward = fwd_ref[...]
    t_fwd[0:2 * bins, :] = table3(forward * ka_row)
    t_fwd[2 * bins:4 * bins, :] = table3(forward * kb_row)
    t_fwd[4 * bins:, :] = table3(pair)
    t_gain[...] = table3(gain_ref[...])
    t_lam[...] = table3(forward)
    lag = lag_ref[...]
    ka_col2 = jnp.concatenate([ka_col, ka_col], axis=1)
    kb_col2 = jnp.concatenate([kb_col, kb_col], axis=1)
    t_lag[:, :6 * bins] = table3(ka_col2 * lag)
    t_lag[:, 6 * bins:12 * bins] = table3(kb_col2 * lag)
    t_lag[:, 12 * bins:] = table3(-pair)

    fetches[1].wait()
    fetches[6].wait()
    wide_adj[...] = adj[...].astype(F32)

    wait_y(first_y)
    for copy in first_x:
        copy.wait()

    ux_next = jnp.concatenate([ux[1:], state[width_x + 1, bins:bins + 1, :]], axis=0)
    bx_next = jnp.concatenate([bx[1:], state[width_x + 1, bins + 1:bins + 2, :]], axis=0)
    last_lane = lane_x == width_y - 1
    uy_next = jnp.where(
        last_lane, pltpu.roll(y_recv[1, bins:bins + width_x, :], width_y - 1, 1), pltpu.roll(uy, width_y - 1, 1))
    by_next = jnp.where(
        last_lane, pltpu.roll(y_recv[1, bins + width_x:, :], width_y - 1, 1), pltpu.roll(by, width_y - 1, 1))
    centre = 1.0 - bx - ux_next - by - uy_next
    for index, values in enumerate((centre, ux, bx, ux_next, bx_next, uy, by, uy_next, by_next)):
        faces[index] = values

    def stencil(field, halo, x, low_x, high_x, low_y, high_y):
        slab = field[x + 1, :bins, :]
        before = jnp.where(lane == 0, pltpu.roll(halo[0, :bins, :], (width_y - x) % width_y, 1), pltpu.roll(slab, 1, 1))
        after = jnp.where(
            lane == width_y - 1, pltpu.roll(halo[1, :bins, :], width_y - 1 - x, 1), pltpu.roll(slab, width_y - 1, 1))
        row = lambda k: faces[k, x:x + 1, :]
        return (
            slab * row(0)
            + row(low_x) * field[x, :bins, :]
            + row(high_x) * field[x + 2, :bins, :]
            + row(low_y) * before
            + row(high_y) * after
        )

    for x in range(width_x):
        moved[x] = stencil(state, y_recv, x, 1, 4, 5, 8)
        lam[x + 1, :bins, :] = wide_adj[pl.ds(x, bins, stride=width_x), :]

    lam[1, bins:, :] = jnp.zeros((8, width_y), F32)
    lam[width_x, bins:, :] = jnp.zeros((8, width_y), F32)
    half, quarter = width_x // 2, width_x // 4
    second_x = x_copies(lam, 4)

    def second_y(group):
        return y_copies(z_send.at[group], z_recv.at[group], 6 + 2 * group)

    @pl.loop(0, 2)
    def _(group):
        places = [p + quarter * group for p in range(quarter)]
        places += [p + half - quarter * group for p in range(quarter, half)]
        current = jnp.concatenate([moved[x] for x in places], axis=1)
        start = jnp.concatenate([lam[x + 1, :bins, :] for x in places], axis=1)
        saved = []
        for step in range(SUBSTEPS):
            spectra = dot(t_fwd[...], stacked(current))
            loss = spectra[4 * bins:]
            saved.append((current, spectra, loss))
            if step < SUBSTEPS - 1:
                both = product(spectra[:2 * bins], spectra[2 * bins:4 * bins])
                current = current + dot(t_gain[...], stacked(both)) - current * loss
        adjoint = start
        for step in reversed(range(SUBSTEPS)):
            current, spectra, loss = saved[step]
            spectra_l = dot(t_lam[...], stacked(adjoint))
            with_b = product_conj(spectra_l, spectra[2 * bins:4 * bins])
            with_a = product_conj(spectra_l, spectra[:2 * bins])
            terms = jnp.concatenate([stacked(with_b), stacked(with_a), stacked(adjoint * current)], axis=0)
            adjoint = adjoint + dot(t_lag[...], terms) - adjoint * loss
        on = jnp.concatenate([active[pl.ds(x, 1), :] for x in places], axis=1) == 1
        result = jnp.where(on, adjoint, start)
        for index, x in enumerate(places):
            lam[x + 1, :bins, :] = result[:, index * width_y:(index + 1) * width_y]

        @pl.when(group == 0)
        def _():
            for copy in second_x:
                copy.start()

        z_send[group, 0], z_send[group, 1] = edges(lam, places)
        start_y(second_y(group), z_recv.at[group])

    outer = [*range(quarter), *range(half + quarter, width_x)]
    for copy in second_x:
        copy.wait()
    writes = []
    for group, places in enumerate((outer, range(quarter, half + quarter))):
        wait_y(second_y(group))
        for x in places:
            moved[x] = stencil(lam, z_recv.at[group], x, 2, 3, 6, 7)
            writes.append(pltpu.make_async_copy(moved.at[x], out.at[:, x, :], out_sem.at[x]))
            writes[-1].start()
    for copy in writes:
        copy.wait()


def body(n_gx, n_gy, concentration, adjoint_next, sign_x, sign_y, courant_x, courant_y, active, kernel_a, kernel_b):
    bins, width_x, width_y = concentration.shape
    rows = bins * width_x
    tables = dft_tables(bins)
    operands = (
        concentration.reshape(rows, width_y),
        adjoint_next.reshape(rows, width_y),
        sign_x, sign_y, courant_x, courant_y, active,
        kernel_a.reshape(1, bins), kernel_b.reshape(1, bins),
        *(jnp.asarray(t) for t in tables),
    )
    return pl.pallas_call(
        functools.partial(kernel, n_gx, n_gy, width_x),
        out_shape=jax.ShapeDtypeStruct((bins, width_x, width_y), F32),
        in_specs=[pl.BlockSpec(memory_space=pltpu.HBM)] * 12,
        out_specs=pl.BlockSpec(memory_space=pltpu.HBM),
        scratch_shapes=[
            *(pltpu.VMEM(a.shape, a.dtype) for a in operands),
            pltpu.VMEM((rows, width_y), F32),
            pltpu.VMEM((rows, width_y), F32),
            pltpu.VMEM((width_x + 2, bins + 8, width_y), F32),
            pltpu.VMEM((width_x + 2, bins + 8, width_y), F32),
            pltpu.VMEM((2, bins + 2 * width_x, width_y), F32),
            pltpu.VMEM((2, bins + 2 * width_x, width_y), F32),
            pltpu.VMEM((2, 2, bins, width_y), F32),
            pltpu.VMEM((2, 2, bins, width_y), F32),
            pltpu.VMEM((width_x, bins, width_y), F32),
            pltpu.VMEM((9, width_x, width_y), F32),
            pltpu.VMEM((5 * bins, 3 * bins), BF16),
            pltpu.VMEM((bins, 6 * bins), BF16),
            pltpu.VMEM((2 * bins, 3 * bins), BF16),
            pltpu.VMEM((bins, 15 * bins), BF16),
            pltpu.SemaphoreType.DMA((10,)),
            pltpu.SemaphoreType.DMA((10,)),
            pltpu.SemaphoreType.DMA((12,)),
            pltpu.SemaphoreType.DMA((width_x,)),
        ],
        compiler_params=pltpu.CompilerParams(
            collective_id=0, has_side_effects=True, vmem_limit_bytes=60 * 1024 * 1024
        ),
    )(*operands)


def solution(mesh):
    return jax.shard_map(
        functools.partial(body, mesh.shape["gx"], mesh.shape["gy"]),
        mesh=mesh,
        in_specs=(
            P(None, "gx", "gy"),
            P(None, "gx", "gy"),
            P("gx", "gy"),
            P("gx", "gy"),
            P("gx", "gy"),
            P("gx", "gy"),
            P("gx", "gy"),
            P(),
            P(),
        ),
        out_specs=P(None, "gx", "gy"),
        check_vma=False,
    )
```

```python
import functools

import jax
import jax.numpy as jnp
import numpy as np
from jax import lax
from jax.experimental import pallas as pl
from jax.experimental.pallas import tpu as pltpu
from jax.sharding import PartitionSpec as P

SUBSTEPS = 4
F32 = jnp.float32
BF16 = jnp.bfloat16


def dft_tables(bins):
    freq = 2 * np.arange(bins) + 1
    index = np.arange(bins)
    angle = np.pi * (freq[:, None] * index[None, :] % (4 * bins)) / (2 * bins)
    forward = np.concatenate([np.cos(angle), -np.sin(angle)], axis=0)

    def inverse(outputs):
        phase = np.pi * (outputs[:, None] * freq[None, :] % (4 * bins)) / (2 * bins)
        return np.concatenate([np.cos(phase), -np.sin(phase)], axis=1) / bins

    gain = inverse(index - 1) * (index > 0)[:, None]
    lag = inverse(index + 1)
    return tuple(np.asarray(t, np.float32) for t in (forward, gain, lag))


def split(values):
    high = values.astype(BF16)
    low = (values - high.astype(F32)).astype(BF16)
    return high, low


def stacked(values):
    high, low = split(values)
    return jnp.concatenate([high, low, high], axis=0)


def table3(values):
    high, low = split(values)
    return jnp.concatenate([high, high, low], axis=1)


def dot(table, values):
    return jnp.dot(table, values, preferred_element_type=F32)


def product(left, right):
    half = left.shape[0] // 2
    lr, li, rr, ri = left[:half], left[half:], right[:half], right[half:]
    return jnp.concatenate([lr * rr - li * ri, lr * ri + li * rr], axis=0)


def product_conj(left, right):
    half = left.shape[0] // 2
    lr, li, rr, ri = left[:half], left[half:], right[:half], right[half:]
    return jnp.concatenate([lr * rr + li * ri, li * rr - lr * ri], axis=0)


def kernel(
    n_gx, n_gy, width_x,
    *refs,
):
    inputs, refs = refs[:12], refs[12:]
    out, refs = refs[0], refs[1:]
    fetched, refs = refs[:12], refs[12:]
    conc, adj, sx, sy, cx, cy, active, ka_ref, kb_ref, fwd_ref, gain_ref, lag_ref = fetched
    (wide, wide_adj, state, lam, y_send, y_recv, z_send, z_recv, moved, faces, t_fwd, t_gain, t_lam, t_lag,
     send_sem, recv_sem, in_sem) = refs
    fetches = [pltpu.make_async_copy(i, f, in_sem.at[k]) for k, (i, f) in enumerate(zip(inputs, fetched))]
    for k in (0, 2, 3, 4, 5, 1, 7, 8, 9, 10, 11, 6):
        fetches[k].start()
    bins = ka_ref.shape[1]
    width_y = sx.shape[1]
    gx = lax.axis_index("gx")
    gy = lax.axis_index("gy")
    nxt_x, prv_x = lax.rem(gx + 1, n_gx), lax.rem(gx + n_gx - 1, n_gx)
    nxt_y, prv_y = jnp.minimum(gy + 1, n_gy - 1), jnp.maximum(gy - 1, 0)
    has_prv, has_nxt = gy > 0, gy < n_gy - 1
    mesh_id = pl.DeviceIdType.MESH

    barrier = pltpu.get_barrier_semaphore()
    pl.semaphore_signal(barrier, inc=1, device_id=(prv_x, gy), device_id_type=mesh_id)
    pl.semaphore_signal(barrier, inc=1, device_id=(nxt_x, gy), device_id_type=mesh_id)

    @pl.when(has_prv)
    def _():
        pl.semaphore_signal(barrier, inc=1, device_id=(gx, prv_y), device_id_type=mesh_id)

    @pl.when(has_nxt)
    def _():
        pl.semaphore_signal(barrier, inc=1, device_id=(gx, nxt_y), device_id_type=mesh_id)

    lane = lax.broadcasted_iota(jnp.int32, (bins, width_y), 1)
    lane_x = lax.broadcasted_iota(jnp.int32, (width_x, width_y), 1)

    for k in (2, 3, 4, 5):
        fetches[k].wait()
    plus_x = sx[...].astype(F32)
    plus_y = sy[...].astype(F32)
    inside = (lane_x + gy * width_y > 0).astype(F32)
    ux = cx[...] * plus_x
    bx = cx[...] * (1.0 - plus_x)
    uy = cy[...] * plus_y * inside
    by = cy[...] * (1.0 - plus_y) * inside

    fetches[0].wait()
    wide[...] = conc[...].astype(F32)
    for x in (0, width_x - 1):
        state[x + 1, :bins, :] = wide[pl.ds(x, bins, stride=width_x), :]
    state[1, bins:bins + 1, :] = ux[0:1]
    state[1, bins + 1:bins + 2, :] = bx[0:1]
    state[1, bins + 2:, :] = jnp.zeros((6, width_y), F32)
    state[width_x, bins:, :] = jnp.zeros((8, width_y), F32)

    def x_copies(field, base):
        return (
            pltpu.make_async_remote_copy(
                src_ref=field.at[1], dst_ref=field.at[width_x + 1],
                send_sem=send_sem.at[base], recv_sem=recv_sem.at[base],
                device_id=(prv_x, gy), device_id_type=mesh_id),
            pltpu.make_async_remote_copy(
                src_ref=field.at[width_x], dst_ref=field.at[0],
                send_sem=send_sem.at[base + 1], recv_sem=recv_sem.at[base + 1],
                device_id=(nxt_x, gy), device_id_type=mesh_id),
        )

    pl.semaphore_wait(barrier, 2 + has_prv.astype(jnp.int32) + has_nxt.astype(jnp.int32))
    first_x = x_copies(state, 0)
    for copy in first_x:
        copy.start()
    for x in range(1, width_x - 1):
        state[x + 1, :bins, :] = wide[pl.ds(x, bins, stride=width_x), :]

    def edges(field, places):
        to_prv = jnp.zeros((bins, width_y), F32)
        to_nxt = jnp.zeros((bins, width_y), F32)
        for x in places:
            slab = field[x + 1, :bins, :]
            to_prv = jnp.where(lane == x, pltpu.roll(slab, x, 1), to_prv)
            to_nxt = jnp.where(lane == x, pltpu.roll(slab, x + 1, 1), to_nxt)
        return to_prv, to_nxt

    y_send[0, :bins, :], y_send[1, :bins, :] = edges(state, range(width_x))
    y_send[0, bins:bins + width_x, :] = uy
    y_send[0, bins + width_x:, :] = by
    y_send[1, bins:, :] = jnp.zeros((2 * width_x, width_y), F32)

    def y_copies(source, target, base):
        return (
            pltpu.make_async_remote_copy(
                src_ref=source.at[0], dst_ref=target.at[1],
                send_sem=send_sem.at[base], recv_sem=recv_sem.at[base],
                device_id=(gx, prv_y), device_id_type=mesh_id),
            pltpu.make_async_remote_copy(
                src_ref=source.at[1], dst_ref=target.at[0],
                send_sem=send_sem.at[base + 1], recv_sem=recv_sem.at[base + 1],
                device_id=(gx, nxt_y), device_id_type=mesh_id),
        )

    def start_y(copies, target):
        to_prv, to_nxt = copies

        @pl.when(has_prv)
        def _():
            to_prv.start()

        @pl.when(has_nxt)
        def _():
            to_nxt.start()

        @pl.when(jnp.logical_not(has_prv))
        def _():
            target[0] = jnp.zeros(target.shape[1:], F32)

        @pl.when(jnp.logical_not(has_nxt))
        def _():
            target[1] = jnp.zeros(target.shape[1:], F32)

    def wait_y(copies):
        to_prv, to_nxt = copies

        @pl.when(has_prv)
        def _():
            to_prv.wait_send()
            to_nxt.wait_recv()

        @pl.when(has_nxt)
        def _():
            to_nxt.wait_send()
            to_prv.wait_recv()

    first_y = y_copies(y_send, y_recv, 2)
    start_y(first_y, y_recv)

    for k in (7, 8, 9, 10, 11):
        fetches[k].wait()
    ka_row, kb_row = ka_ref[...], kb_ref[...]
    ka_full = jnp.broadcast_to(ka_row, (bins, bins))
    kb_full = jnp.broadcast_to(kb_row, (bins, bins))
    ka_col, kb_col = ka_full.T, kb_full.T
    pair = ka_col * kb_full + kb_col * ka_full
    forward = fwd_ref[...]
    t_fwd[0:2 * bins, :] = table3(forward * ka_row)
    t_fwd[2 * bins:4 * bins, :] = table3(forward * kb_row)
    t_fwd[4 * bins:, :] = table3(pair)
    t_gain[...] = table3(gain_ref[...])
    t_lam[...] = table3(forward)
    lag = lag_ref[...]
    ka_col2 = jnp.concatenate([ka_col, ka_col], axis=1)
    kb_col2 = jnp.concatenate([kb_col, kb_col], axis=1)
    t_lag[:, :6 * bins] = table3(ka_col2 * lag)
    t_lag[:, 6 * bins:12 * bins] = table3(kb_col2 * lag)
    t_lag[:, 12 * bins:] = table3(-pair)

    fetches[1].wait()
    fetches[6].wait()
    wide_adj[...] = adj[...].astype(F32)

    wait_y(first_y)
    for copy in first_x:
        copy.wait()

    ux_next = jnp.concatenate([ux[1:], state[width_x + 1, bins:bins + 1, :]], axis=0)
    bx_next = jnp.concatenate([bx[1:], state[width_x + 1, bins + 1:bins + 2, :]], axis=0)
    last_lane = lane_x == width_y - 1
    uy_next = jnp.where(
        last_lane, pltpu.roll(y_recv[1, bins:bins + width_x, :], width_y - 1, 1), pltpu.roll(uy, width_y - 1, 1))
    by_next = jnp.where(
        last_lane, pltpu.roll(y_recv[1, bins + width_x:, :], width_y - 1, 1), pltpu.roll(by, width_y - 1, 1))
    centre = 1.0 - bx - ux_next - by - uy_next
    for index, values in enumerate((centre, ux, bx, ux_next, bx_next, uy, by, uy_next, by_next)):
        faces[index] = values

    def stencil(field, halo, x, low_x, high_x, low_y, high_y):
        slab = field[x + 1, :bins, :]
        before = jnp.where(lane == 0, pltpu.roll(halo[0, :bins, :], (width_y - x) % width_y, 1), pltpu.roll(slab, 1, 1))
        after = jnp.where(
            lane == width_y - 1, pltpu.roll(halo[1, :bins, :], width_y - 1 - x, 1), pltpu.roll(slab, width_y - 1, 1))
        row = lambda k: faces[k, x:x + 1, :]
        return (
            slab * row(0)
            + row(low_x) * field[x, :bins, :]
            + row(high_x) * field[x + 2, :bins, :]
            + row(low_y) * before
            + row(high_y) * after
        )

    for x in range(width_x):
        moved[x] = stencil(state, y_recv, x, 1, 4, 5, 8)
        lam[x + 1, :bins, :] = wide_adj[pl.ds(x, bins, stride=width_x), :]

    lam[1, bins:, :] = jnp.zeros((8, width_y), F32)
    lam[width_x, bins:, :] = jnp.zeros((8, width_y), F32)
    half, quarter = width_x // 2, width_x // 4
    second_x = x_copies(lam, 4)

    def second_y(group):
        return y_copies(z_send.at[group], z_recv.at[group], 6 + 2 * group)

    @pl.loop(0, 2)
    def _(group):
        places = [p + quarter * group for p in range(quarter)]
        places += [p + half - quarter * group for p in range(quarter, half)]
        current = jnp.concatenate([moved[x] for x in places], axis=1)
        start = jnp.concatenate([lam[x + 1, :bins, :] for x in places], axis=1)
        saved = []
        for step in range(SUBSTEPS):
            spectra = dot(t_fwd[...], stacked(current))
            loss = spectra[4 * bins:]
            saved.append((current, spectra, loss))
            if step < SUBSTEPS - 1:
                both = product(spectra[:2 * bins], spectra[2 * bins:4 * bins])
                current = current + dot(t_gain[...], stacked(both)) - current * loss
        adjoint = start
        for step in reversed(range(SUBSTEPS)):
            current, spectra, loss = saved[step]
            spectra_l = dot(t_lam[...], stacked(adjoint))
            with_b = product_conj(spectra_l, spectra[2 * bins:4 * bins])
            with_a = product_conj(spectra_l, spectra[:2 * bins])
            terms = jnp.concatenate([stacked(with_b), stacked(with_a), stacked(adjoint * current)], axis=0)
            adjoint = adjoint + dot(t_lag[...], terms) - adjoint * loss
        on = jnp.concatenate([active[pl.ds(x, 1), :] for x in places], axis=1) == 1
        result = jnp.where(on, adjoint, start)
        for index, x in enumerate(places):
            lam[x + 1, :bins, :] = result[:, index * width_y:(index + 1) * width_y]

        @pl.when(group == 0)
        def _():
            for copy in second_x:
                copy.start()

        z_send[group, 0], z_send[group, 1] = edges(lam, places)
        start_y(second_y(group), z_recv.at[group])

    outer = [*range(quarter), *range(half + quarter, width_x)]
    for copy in second_x:
        copy.wait()
    for group, places in enumerate((outer, range(quarter, half + quarter))):
        wait_y(second_y(group))
        for x in places:
            out[pl.ds(x, bins, stride=width_x), :] = stencil(lam, z_recv.at[group], x, 2, 3, 6, 7)


def body(n_gx, n_gy, concentration, adjoint_next, sign_x, sign_y, courant_x, courant_y, active, kernel_a, kernel_b):
    bins, width_x, width_y = concentration.shape
    rows = bins * width_x
    tables = dft_tables(bins)
    operands = (
        concentration.reshape(rows, width_y),
        adjoint_next.reshape(rows, width_y),
        sign_x, sign_y, courant_x, courant_y, active,
        kernel_a.reshape(1, bins), kernel_b.reshape(1, bins),
        *(jnp.asarray(t) for t in tables),
    )
    result = pl.pallas_call(
        functools.partial(kernel, n_gx, n_gy, width_x),
        out_shape=pltpu.VMEM((rows, width_y), F32),
        in_specs=[pl.BlockSpec(memory_space=pltpu.HBM)] * 12,
        out_specs=pl.BlockSpec(memory_space=pltpu.VMEM),
        scratch_shapes=[
            *(pltpu.VMEM(a.shape, a.dtype) for a in operands),
            pltpu.VMEM((rows, width_y), F32),
            pltpu.VMEM((rows, width_y), F32),
            pltpu.VMEM((width_x + 2, bins + 8, width_y), F32),
            pltpu.VMEM((width_x + 2, bins + 8, width_y), F32),
            pltpu.VMEM((2, bins + 2 * width_x, width_y), F32),
            pltpu.VMEM((2, bins + 2 * width_x, width_y), F32),
            pltpu.VMEM((2, 2, bins, width_y), F32),
            pltpu.VMEM((2, 2, bins, width_y), F32),
            pltpu.VMEM((width_x, bins, width_y), F32),
            pltpu.VMEM((9, width_x, width_y), F32),
            pltpu.VMEM((5 * bins, 3 * bins), BF16),
            pltpu.VMEM((bins, 6 * bins), BF16),
            pltpu.VMEM((2 * bins, 3 * bins), BF16),
            pltpu.VMEM((bins, 15 * bins), BF16),
            pltpu.SemaphoreType.DMA((10,)),
            pltpu.SemaphoreType.DMA((10,)),
            pltpu.SemaphoreType.DMA((12,)),
        ],
        compiler_params=pltpu.CompilerParams(
            collective_id=0, has_side_effects=True, vmem_limit_bytes=60 * 1024 * 1024
        ),
    )(*operands)
    return result.reshape(bins, width_x, width_y)


def solution(mesh):
    return jax.shard_map(
        functools.partial(body, mesh.shape["gx"], mesh.shape["gy"]),
        mesh=mesh,
        in_specs=(
            P(None, "gx", "gy"),
            P(None, "gx", "gy"),
            P("gx", "gy"),
            P("gx", "gy"),
            P("gx", "gy"),
            P("gx", "gy"),
            P("gx", "gy"),
            P(),
            P(),
        ),
        out_specs=P(None, "gx", "gy"),
        check_vma=False,
    )
```

```python
import functools

import jax
import jax.numpy as jnp
import numpy as np
from jax import lax
from jax.experimental import pallas as pl
from jax.experimental.pallas import tpu as pltpu
from jax.sharding import PartitionSpec as P

SUBSTEPS = 4
F32 = jnp.float32
BF16 = jnp.bfloat16


def dft_tables(bins):
    freq = 2 * np.arange(bins) + 1
    index = np.arange(bins)
    angle = np.pi * (freq[:, None] * index[None, :] % (4 * bins)) / (2 * bins)
    forward = np.concatenate([np.cos(angle), -np.sin(angle)], axis=0)

    def inverse(outputs):
        phase = np.pi * (outputs[:, None] * freq[None, :] % (4 * bins)) / (2 * bins)
        return np.concatenate([np.cos(phase), -np.sin(phase)], axis=1) / bins

    gain = inverse(index - 1) * (index > 0)[:, None]
    lag = inverse(index + 1)
    return tuple(np.asarray(t, np.float32) for t in (forward, gain, lag))


def split(values):
    high = values.astype(BF16)
    low = (values - high.astype(F32)).astype(BF16)
    return high, low


def stacked(values):
    high, low = split(values)
    return jnp.concatenate([high, low, high], axis=0)


def table3(values):
    high, low = split(values)
    return jnp.concatenate([high, high, low], axis=1)


def dot(table, values):
    return jnp.dot(table, values, preferred_element_type=F32)


def product(left, right):
    half = left.shape[0] // 2
    lr, li, rr, ri = left[:half], left[half:], right[:half], right[half:]
    return jnp.concatenate([lr * rr - li * ri, lr * ri + li * rr], axis=0)


def product_conj(left, right):
    half = left.shape[0] // 2
    lr, li, rr, ri = left[:half], left[half:], right[:half], right[half:]
    return jnp.concatenate([lr * rr + li * ri, li * rr - lr * ri], axis=0)


def kernel(
    n_gx, n_gy, width_x,
    *refs,
):
    inputs, refs = refs[:12], refs[12:]
    out, refs = refs[0], refs[1:]
    fetched, refs = refs[:12], refs[12:]
    conc, adj, sx, sy, cx, cy, active, ka_ref, kb_ref, fwd_ref, gain_ref, lag_ref = fetched
    (wide, wide_adj, state, lam, y_send, y_recv, z_send, z_recv, moved, faces, t_fwd, t_gain, t_lam, t_lag,
     send_sem, recv_sem, in_sem) = refs
    fetches = [pltpu.make_async_copy(i, f, in_sem.at[k]) for k, (i, f) in enumerate(zip(inputs, fetched))]
    for k in (0, 2, 3, 4, 5, 1, 7, 8, 9, 10, 11, 6):
        fetches[k].start()
    bins = ka_ref.shape[1]
    width_y = sx.shape[1]
    gx = lax.axis_index("gx")
    gy = lax.axis_index("gy")
    nxt_x, prv_x = lax.rem(gx + 1, n_gx), lax.rem(gx + n_gx - 1, n_gx)
    nxt_y, prv_y = jnp.minimum(gy + 1, n_gy - 1), jnp.maximum(gy - 1, 0)
    has_prv, has_nxt = gy > 0, gy < n_gy - 1
    mesh_id = pl.DeviceIdType.MESH

    barrier = pltpu.get_barrier_semaphore()
    pl.semaphore_signal(barrier, inc=1, device_id=(prv_x, gy), device_id_type=mesh_id)
    pl.semaphore_signal(barrier, inc=1, device_id=(nxt_x, gy), device_id_type=mesh_id)

    @pl.when(has_prv)
    def _():
        pl.semaphore_signal(barrier, inc=1, device_id=(gx, prv_y), device_id_type=mesh_id)

    @pl.when(has_nxt)
    def _():
        pl.semaphore_signal(barrier, inc=1, device_id=(gx, nxt_y), device_id_type=mesh_id)

    lane = lax.broadcasted_iota(jnp.int32, (bins, width_y), 1)
    lane_x = lax.broadcasted_iota(jnp.int32, (width_x, width_y), 1)

    for k in (2, 3, 4, 5):
        fetches[k].wait()
    plus_x = sx[...].astype(F32)
    plus_y = sy[...].astype(F32)
    inside = (lane_x + gy * width_y > 0).astype(F32)
    ux = cx[...] * plus_x
    bx = cx[...] * (1.0 - plus_x)
    uy = cy[...] * plus_y * inside
    by = cy[...] * (1.0 - plus_y) * inside

    fetches[0].wait()
    wide[...] = conc[...].astype(F32)
    for x in (0, width_x - 1):
        state[x + 1, :bins, :] = wide[pl.ds(x, bins, stride=width_x), :]
    state[1, bins:bins + 1, :] = ux[0:1]
    state[1, bins + 1:bins + 2, :] = bx[0:1]
    state[1, bins + 2:, :] = jnp.zeros((6, width_y), F32)
    state[width_x, bins:, :] = jnp.zeros((8, width_y), F32)

    def x_copies(field, base):
        return (
            pltpu.make_async_remote_copy(
                src_ref=field.at[1], dst_ref=field.at[width_x + 1],
                send_sem=send_sem.at[base], recv_sem=recv_sem.at[base],
                device_id=(prv_x, gy), device_id_type=mesh_id),
            pltpu.make_async_remote_copy(
                src_ref=field.at[width_x], dst_ref=field.at[0],
                send_sem=send_sem.at[base + 1], recv_sem=recv_sem.at[base + 1],
                device_id=(nxt_x, gy), device_id_type=mesh_id),
        )

    pl.semaphore_wait(barrier, 2 + has_prv.astype(jnp.int32) + has_nxt.astype(jnp.int32))
    first_x = x_copies(state, 0)
    for copy in first_x:
        copy.start()
    for x in range(1, width_x - 1):
        state[x + 1, :bins, :] = wide[pl.ds(x, bins, stride=width_x), :]

    def edges(field, places):
        to_prv = jnp.zeros((bins, width_y), F32)
        to_nxt = jnp.zeros((bins, width_y), F32)
        for x in places:
            slab = field[x + 1, :bins, :]
            to_prv = jnp.where(lane == x, pltpu.roll(slab, x, 1), to_prv)
            to_nxt = jnp.where(lane == x, pltpu.roll(slab, x + 1, 1), to_nxt)
        return to_prv, to_nxt

    y_send[0, :bins, :], y_send[1, :bins, :] = edges(state, range(width_x))
    y_send[0, bins:bins + width_x, :] = uy
    y_send[0, bins + width_x:, :] = by
    y_send[1, bins:, :] = jnp.zeros((2 * width_x, width_y), F32)

    def y_copies(source, target, base):
        return (
            pltpu.make_async_remote_copy(
                src_ref=source.at[0], dst_ref=target.at[1],
                send_sem=send_sem.at[base], recv_sem=recv_sem.at[base],
                device_id=(gx, prv_y), device_id_type=mesh_id),
            pltpu.make_async_remote_copy(
                src_ref=source.at[1], dst_ref=target.at[0],
                send_sem=send_sem.at[base + 1], recv_sem=recv_sem.at[base + 1],
                device_id=(gx, nxt_y), device_id_type=mesh_id),
        )

    def start_y(copies, target):
        to_prv, to_nxt = copies

        @pl.when(has_prv)
        def _():
            to_prv.start()

        @pl.when(has_nxt)
        def _():
            to_nxt.start()

        @pl.when(jnp.logical_not(has_prv))
        def _():
            target[0] = jnp.zeros(target.shape[1:], F32)

        @pl.when(jnp.logical_not(has_nxt))
        def _():
            target[1] = jnp.zeros(target.shape[1:], F32)

    def wait_y(copies):
        to_prv, to_nxt = copies

        @pl.when(has_prv)
        def _():
            to_prv.wait_send()
            to_nxt.wait_recv()

        @pl.when(has_nxt)
        def _():
            to_nxt.wait_send()
            to_prv.wait_recv()

    first_y = y_copies(y_send, y_recv, 2)
    start_y(first_y, y_recv)

    for k in (7, 8, 9, 10, 11):
        fetches[k].wait()
    ka_row, kb_row = ka_ref[...], kb_ref[...]
    ka_full = jnp.broadcast_to(ka_row, (bins, bins))
    kb_full = jnp.broadcast_to(kb_row, (bins, bins))
    ka_col, kb_col = ka_full.T, kb_full.T
    pair = ka_col * kb_full + kb_col * ka_full
    forward = fwd_ref[...]
    t_fwd[0:2 * bins, :] = table3(forward * ka_row)
    t_fwd[2 * bins:4 * bins, :] = table3(forward * kb_row)
    t_fwd[4 * bins:, :] = table3(pair)
    t_gain[...] = table3(gain_ref[...])
    t_lam[...] = table3(forward)
    lag = lag_ref[...]
    ka_col2 = jnp.concatenate([ka_col, ka_col], axis=1)
    kb_col2 = jnp.concatenate([kb_col, kb_col], axis=1)
    t_lag[:, :6 * bins] = table3(ka_col2 * lag)
    t_lag[:, 6 * bins:12 * bins] = table3(kb_col2 * lag)
    t_lag[:, 12 * bins:] = table3(-pair)

    fetches[1].wait()
    fetches[6].wait()
    wide_adj[...] = adj[...].astype(F32)
    for x in range(width_x):
        lam[x + 1, :bins, :] = wide_adj[pl.ds(x, bins, stride=width_x), :]

    wait_y(first_y)
    for copy in first_x:
        copy.wait()

    ux_next = jnp.concatenate([ux[1:], state[width_x + 1, bins:bins + 1, :]], axis=0)
    bx_next = jnp.concatenate([bx[1:], state[width_x + 1, bins + 1:bins + 2, :]], axis=0)
    last_lane = lane_x == width_y - 1
    uy_next = jnp.where(
        last_lane, pltpu.roll(y_recv[1, bins:bins + width_x, :], width_y - 1, 1), pltpu.roll(uy, width_y - 1, 1))
    by_next = jnp.where(
        last_lane, pltpu.roll(y_recv[1, bins + width_x:, :], width_y - 1, 1), pltpu.roll(by, width_y - 1, 1))
    centre = 1.0 - bx - ux_next - by - uy_next
    for index, values in enumerate((centre, ux, bx, ux_next, bx_next, uy, by, uy_next, by_next)):
        faces[index] = values

    def stencil(field, halo, x, low_x, high_x, low_y, high_y):
        slab = field[x + 1, :bins, :]
        before = jnp.where(lane == 0, pltpu.roll(halo[0, :bins, :], (width_y - x) % width_y, 1), pltpu.roll(slab, 1, 1))
        after = jnp.where(
            lane == width_y - 1, pltpu.roll(halo[1, :bins, :], width_y - 1 - x, 1), pltpu.roll(slab, width_y - 1, 1))
        row = lambda k: faces[k, x:x + 1, :]
        return (
            slab * row(0)
            + row(low_x) * field[x, :bins, :]
            + row(high_x) * field[x + 2, :bins, :]
            + row(low_y) * before
            + row(high_y) * after
        )

    for x in range(width_x):
        moved[x] = stencil(state, y_recv, x, 1, 4, 5, 8)

    lam[1, bins:, :] = jnp.zeros((8, width_y), F32)
    lam[width_x, bins:, :] = jnp.zeros((8, width_y), F32)
    half, quarter = width_x // 2, width_x // 4
    second_x = x_copies(lam, 4)

    def second_y(group):
        return y_copies(z_send.at[group], z_recv.at[group], 6 + 2 * group)

    @pl.loop(0, 2)
    def _(group):
        places = [p + quarter * group for p in range(quarter)]
        places += [p + half - quarter * group for p in range(quarter, half)]
        current = jnp.concatenate([moved[x] for x in places], axis=1)
        start = jnp.concatenate([lam[x + 1, :bins, :] for x in places], axis=1)
        saved = []
        for step in range(SUBSTEPS):
            spectra = dot(t_fwd[...], stacked(current))
            loss = spectra[4 * bins:]
            saved.append((current, spectra, loss))
            if step < SUBSTEPS - 1:
                both = product(spectra[:2 * bins], spectra[2 * bins:4 * bins])
                current = current + dot(t_gain[...], stacked(both)) - current * loss
        adjoint = start
        for step in reversed(range(SUBSTEPS)):
            current, spectra, loss = saved[step]
            spectra_l = dot(t_lam[...], stacked(adjoint))
            with_b = product_conj(spectra_l, spectra[2 * bins:4 * bins])
            with_a = product_conj(spectra_l, spectra[:2 * bins])
            terms = jnp.concatenate([stacked(with_b), stacked(with_a), stacked(adjoint * current)], axis=0)
            adjoint = adjoint + dot(t_lag[...], terms) - adjoint * loss
        on = jnp.concatenate([active[pl.ds(x, 1), :] for x in places], axis=1) == 1
        result = jnp.where(on, adjoint, start)
        for index, x in enumerate(places):
            lam[x + 1, :bins, :] = result[:, index * width_y:(index + 1) * width_y]

        @pl.when(group == 0)
        def _():
            for copy in second_x:
                copy.start()

        z_send[group, 0], z_send[group, 1] = edges(lam, places)
        start_y(second_y(group), z_recv.at[group])

    outer = [*range(quarter), *range(half + quarter, width_x)]
    for copy in second_x:
        copy.wait()
    for group, places in enumerate((outer, range(quarter, half + quarter))):
        wait_y(second_y(group))
        for x in places:
            out[pl.ds(x, bins, stride=width_x), :] = stencil(lam, z_recv.at[group], x, 2, 3, 6, 7)


def body(n_gx, n_gy, concentration, adjoint_next, sign_x, sign_y, courant_x, courant_y, active, kernel_a, kernel_b):
    bins, width_x, width_y = concentration.shape
    rows = bins * width_x
    tables = dft_tables(bins)
    operands = (
        concentration.reshape(rows, width_y),
        adjoint_next.reshape(rows, width_y),
        sign_x, sign_y, courant_x, courant_y, active,
        kernel_a.reshape(1, bins), kernel_b.reshape(1, bins),
        *(jnp.asarray(t) for t in tables),
    )
    result = pl.pallas_call(
        functools.partial(kernel, n_gx, n_gy, width_x),
        out_shape=pltpu.VMEM((rows, width_y), F32),
        in_specs=[pl.BlockSpec(memory_space=pltpu.HBM)] * 12,
        out_specs=pl.BlockSpec(memory_space=pltpu.VMEM),
        scratch_shapes=[
            *(pltpu.VMEM(a.shape, a.dtype) for a in operands),
            pltpu.VMEM((rows, width_y), F32),
            pltpu.VMEM((rows, width_y), F32),
            pltpu.VMEM((width_x + 2, bins + 8, width_y), F32),
            pltpu.VMEM((width_x + 2, bins + 8, width_y), F32),
            pltpu.VMEM((2, bins + 2 * width_x, width_y), F32),
            pltpu.VMEM((2, bins + 2 * width_x, width_y), F32),
            pltpu.VMEM((2, 2, bins, width_y), F32),
            pltpu.VMEM((2, 2, bins, width_y), F32),
            pltpu.VMEM((width_x, bins, width_y), F32),
            pltpu.VMEM((9, width_x, width_y), F32),
            pltpu.VMEM((5 * bins, 3 * bins), BF16),
            pltpu.VMEM((bins, 6 * bins), BF16),
            pltpu.VMEM((2 * bins, 3 * bins), BF16),
            pltpu.VMEM((bins, 15 * bins), BF16),
            pltpu.SemaphoreType.DMA((10,)),
            pltpu.SemaphoreType.DMA((10,)),
            pltpu.SemaphoreType.DMA((12,)),
        ],
        compiler_params=pltpu.CompilerParams(
            collective_id=0, has_side_effects=True, vmem_limit_bytes=60 * 1024 * 1024
        ),
    )(*operands)
    return result.reshape(bins, width_x, width_y)


def solution(mesh):
    return jax.shard_map(
        functools.partial(body, mesh.shape["gx"], mesh.shape["gy"]),
        mesh=mesh,
        in_specs=(
            P(None, "gx", "gy"),
            P(None, "gx", "gy"),
            P("gx", "gy"),
            P("gx", "gy"),
            P("gx", "gy"),
            P("gx", "gy"),
            P("gx", "gy"),
            P(),
            P(),
        ),
        out_specs=P(None, "gx", "gy"),
        check_vma=False,
    )
```
